128 devices in a mesh: group: 8 (over x, core), tile: 16 (over y, z).
Axes of the slice: x: 4, y: 4, z: 4, core: 2. Of those that a mesh axis runs over, the one named last changes fastest.
Arguments:
- embeddings: bfloat16 [32768, 1024], P(('group', 'tile'))
- cluster: int32 [32768], P(('group', 'tile')), may hold values from 0 to 7, as said below
Outputs:
- max_similarity: float32 [32768], P(('group', 'tile'))
The draws below stay inside these ranges and needn't reach their ends.
Inputs may be any that keep to these rules, and one draw needn't show every extreme that they name: Among the 256 documents of one device at most 96 belong to one cluster; on every device some cluster has exactly 96, and one cluster has exactly 96 on every device of some index along tile.
All inputs are finite; a program needn't handle non-finite values.
Results may differ from the reference program's by a relative error of at most 0.00057.
Values may be sent and summed in bfloat16 or wider, within the bound.
A program may use at most 128 MiB of HBM per device.

```python
import math
import jax
import jax.numpy as jnp
from jax import lax

D = 1024
DOC_DEV = 256
CAP = 96
CLUSTERS = 8
DOCS = 32768
N_GROUP = 8
N_TILE = 16


def assign(key):
    blocks = DOCS // DOC_DEV
    groups = CLUSTERS
    columns = blocks // groups
    key_big, key_col, key_pick, key_alt, key_blocks = jax.random.split(key, 5)
    biggest = jax.random.randint(key_big, (), 0, groups).astype(jnp.int32)
    column = jax.random.randint(key_col, (), 0, columns).astype(jnp.int32)
    position = jnp.arange(blocks, dtype=jnp.int32)
    follow = jax.random.randint(key_pick, (blocks,), 0, 4) < 3
    another = jax.random.randint(key_alt, (blocks,), 0, groups).astype(jnp.int32)
    chosen = jnp.where((position % columns == column) | follow, biggest, another)

    def one_block(block_key, leading):
        key_perm, key_shuffle = jax.random.split(block_key)
        others = (leading + 1 + jnp.arange((groups - 1) * CAP, dtype=jnp.int32) // CAP) % groups
        others = jax.random.permutation(key_perm, others)[:DOC_DEV - CAP]
        labels = jnp.concatenate([jnp.full((CAP,), leading, jnp.int32), others])
        return jax.random.permutation(key_shuffle, labels)
    labelled = jax.vmap(one_block)(jax.random.split(key_blocks, blocks), chosen)
    return labelled.reshape(DOCS).astype(jnp.int32)


def draw_cluster(key, part):
    return assign(key)


def draw_embeddings(key, part):
    clusters = assign(key)
    key = jax.random.fold_in(key, 7)
    key_rank = jax.random.fold_in(key, 0)
    key_centre = jax.random.fold_in(key, 1)
    key_noise = jax.random.fold_in(key, 2)
    key_flag = jax.random.fold_in(key, 3)
    key_mix = jax.random.fold_in(key, 4)
    key_scale = jax.random.fold_in(key, 5)
    key_anti = jax.random.fold_in(key, 7)
    rank = jax.random.permutation(key_rank, DOCS).astype(jnp.int32)
    order = jnp.argsort(clusters * DOCS + rank, stable=True).astype(jnp.int32)
    half_docs = DOCS // 2
    noise = jax.random.normal(key_noise, (DOCS, D), jnp.float32)
    centres = jax.random.normal(key_centre, (CLUSTERS, D), jnp.float32)
    weight = 0.3
    scales = jnp.exp(jax.random.uniform(key_scale, (DOCS, 1), jnp.float32, 0.0, 2.3))
    paired = noise.reshape(half_docs, 2, D)
    flagged = jax.random.randint(key_flag, (half_docs, 1), 0, 5) < 1
    mixing = jnp.where(flagged, jax.random.uniform(key_mix, (half_docs, 1), jnp.float32, 0.2, 0.98), 0.0)
    second = mixing * paired[:, 0] + jnp.sqrt(1.0 - mixing * mixing) * paired[:, 1]
    sorted_noise = jnp.stack([paired[:, 0], second], axis=1).reshape(DOCS, D)
    placed = jnp.zeros((DOCS, D), jnp.float32).at[order].set(sorted_noise)
    sorted_clusters = clusters[order]
    leading_sorted = jnp.concatenate([jnp.ones((1,), jnp.bool_), sorted_clusters[1:] != sorted_clusters[:-1]])
    opposed = jnp.zeros((DOCS,), jnp.bool_).at[order].set(leading_sorted)
    centre_part = weight * centres[clusters]
    fresh = jax.random.normal(key_anti, (DOCS, D), jnp.float32)
    regular = centre_part + placed
    contrary = -3.0 * centre_part + 0.2 * fresh
    whole = jnp.where(opposed[:, None], contrary, regular) * scales
    return whole.astype(jnp.bfloat16)


def setup_inputs(seed: int = 0) -> dict:
    arg_keys = jax.random.split(jax.random.key(seed), 3)
    embeddings = draw_embeddings(jax.random.fold_in(arg_keys[2], 71), 0)
    cluster = draw_cluster(jax.random.fold_in(arg_keys[2], 71), 0)
    return {"embeddings": embeddings, "cluster": cluster}


EPS = 1e-06

def reference(embeddings, cluster):
    e32 = embeddings.astype(jnp.float32)
    normed = (e32 * lax.rsqrt(lax.optimization_barrier(jnp.sum(e32 * e32, axis=1, keepdims=True)) + EPS)).astype(jnp.bfloat16)
    width_rows = N_GROUP * N_TILE * CAP
    blk = math.gcd(width_rows, 1024)
    group_of = cluster.astype(jnp.int32)
    order = jnp.argsort(group_of, stable=True).astype(jnp.int32)
    sorted_rows = normed[order].astype(jnp.float32)
    sorted_ids = cluster[order]
    sorted_group = group_of[order]
    member = (group_of[:, None] == jnp.arange(N_GROUP, dtype=jnp.int32)[None, :]).astype(jnp.int32)
    counts = lax.optimization_barrier(jnp.sum(member, axis=0))
    offsets = (jnp.cumsum(counts) - counts).astype(jnp.int32)
    padded_rows = jnp.concatenate([sorted_rows, jnp.zeros((width_rows, sorted_rows.shape[1]), jnp.float32)], 0)
    padded_ids = jnp.concatenate([sorted_ids, jnp.full((width_rows,), -1, jnp.int32)], 0)

    def per_group(start):
        keys = lax.dynamic_slice_in_dim(padded_rows, start, width_rows, 0)
        key_ids = lax.dynamic_slice_in_dim(padded_ids, start, width_rows, 0)
        positions = jnp.arange(width_rows, dtype=jnp.int32)

        def per_block(bstart):
            queries = lax.dynamic_slice_in_dim(keys, bstart, blk, 0)
            query_ids = lax.dynamic_slice_in_dim(key_ids, bstart, blk, 0)
            sims = jnp.dot(queries, keys.T, preferred_element_type=jnp.float32)
            own = bstart + jnp.arange(blk, dtype=jnp.int32)
            mask = (query_ids[:, None] == key_ids[None, :]) & (own[:, None] != positions[None, :])
            return lax.optimization_barrier(jnp.max(jnp.where(mask, sims, jnp.float32(-1.0)), axis=1))
        starts = jnp.arange(width_rows // blk, dtype=jnp.int32) * blk
        return lax.map(per_block, starts).reshape(width_rows)
    results = lax.map(per_group, offsets)
    local = jnp.arange(sorted_group.shape[0], dtype=jnp.int32) - offsets[sorted_group]
    values = results[sorted_group, local]
    return jnp.zeros(values.shape, jnp.float32).at[order].set(values)
```

```python
import functools

import jax
import jax.numpy as jnp
from jax import lax
from jax.experimental import pallas as pl
from jax.experimental.pallas import tpu as pltpu
from jax.sharding import PartitionSpec as P

EPS = 1e-06
MESH = pl.DeviceIdType.MESH

TWIST = ((0, 1, 0), (0, 0, 0), (1, 0, 0))
SLOTS = (
    (0, 0, 0), (1, 0, 0), (0, 1, 0), (0, 0, 1), (3, 0, 1), (1, 3, 0), (0, 1, 3),
    (2, 0, 0), (2, 3, 0), (0, 2, 0), (0, 3, 1), (1, 0, 3), (0, 1, 2),
)
FIRST = ((0, 1, 0), (0, 2, 2), (0, 3, 4), (3, 4, 1), (1, 5, 3), (2, 6, 5))
SECOND = ((1, 7, 0), (5, 8, 1), (2, 9, 2), (3, 10, 3), (1, 11, 4), (6, 12, 5))
EARLY = ((0, (1, 2, 3, 4, 5)), (4, (1, 2, 3, 5)), (5, (1, 2, 3, 6)), (6, (1, 3, 4, 0)))
LATE = ((0, (9, 11, 7)), (2, (12, 8)), (3, (8, 9)), (4, (9, 11, 10, 12)), (5, (12, 11)), (6, (10, 8, 11)))
LAST = ((12, (7, 8)),)
SHARED = (0, 2, 3, 4, 5, 6, 12)

K = len(SLOTS)
CHUNKS = 8
AHEAD = 2


def chi(axis, parities):
    return sum(t * p for t, p in zip(TWIST[axis], parities)) % 2


def kernel(x_ref, cluster_ref, out_ref, buf, cid, rid, rowacc, colacc, outb, inb,
           arrive, shared, ids_in, ids_pair, sent, sent_pair, ids_sent, ids_pair_sent,
           res_in, res_pair_in, res_sent, res_pair_sent):
    rows = x_ref.shape[0]
    part = rows // CHUNKS
    group, tile = lax.axis_index("group"), lax.axis_index("tile")
    core = lax.rem(group, 2)
    here = (group // 2, tile // 4, lax.rem(tile, 4))
    odd = [lax.rem(h, 2) for h in here]
    sign = [1 - 2 * lax.rem(sum(t * o for t, o in zip(TWIST[a], odd)) + 0 * odd[0], 2) for a in range(3)]

    def device(chip, which):
        return (chip[0] * 2 + which, chip[1] * 4 + chip[2])

    def link(which):
        axis, step = which // 2, 1 - 2 * (which % 2)
        chip = list(here)
        chip[axis] = lax.rem(here[axis] + sign[axis] * step + 4, 4)
        return chip

    def owner(slot):
        s = SLOTS[slot]
        flip = [1 - 2 * chi(a, [v % 2 for v in s]) for a in range(3)]
        return [lax.rem(here[a] - sign[a] * (flip[a] * s[a]) + 8, 4) for a in range(3)]

    sibling = device(here, 1 - core)
    links = [device(link(w), core) for w in range(6)]

    barrier = pltpu.get_barrier_semaphore()
    partners = links + [sibling]
    for partner in partners:
        pl.semaphore_signal(barrier, inc=1, device_id=partner, device_id_type=MESH)

    e32 = x_ref[...].astype(jnp.float32)
    normed = e32 * lax.rsqrt(jnp.sum(e32 * e32, axis=1, keepdims=True) + EPS)
    buf[0, core] = normed.astype(jnp.bfloat16)
    cid[0, core] = cluster_ref[...]
    rowacc[...] = jnp.full(rowacc.shape, -1.0, jnp.float32)
    colacc[...] = jnp.full(colacc.shape, -1.0, jnp.float32)

    pl.semaphore_wait(barrier, len(partners))

    def remote(src, dst, send, recv, to):
        return pltpu.make_async_remote_copy(
            src_ref=src, dst_ref=dst, send_sem=send, recv_sem=recv, device_id=to, device_id_type=MESH
        )

    def chunk(edge, n):
        src, dst, which = edge
        piece = pl.ds(n * part, part)
        return remote(buf.at[src, core, piece], buf.at[dst, core, piece], sent.at[dst], arrive.at[dst, n], links[which])

    def across(slot, n):
        piece = pl.ds(n * part, part)
        return remote(buf.at[slot, core, piece], buf.at[slot, core, piece], sent_pair.at[slot], shared.at[slot], sibling)

    def whole(slot):
        return remote(buf.at[slot, core], buf.at[slot, core], sent_pair.at[slot], shared.at[slot], sibling)

    def ids_across():
        return remote(cid.at[0, core], cid.at[0, core], ids_pair_sent, ids_pair, sibling)

    def ids(edge):
        src, dst, which = edge
        return remote(cid.at[src], cid.at[dst], ids_sent.at[dst], ids_in.at[dst], links[which])

    first_of = {e[2]: e for e in FIRST}
    second_of = {e[2]: e for e in SECOND}
    eager = [w for w in range(6) if first_of[w][0] == 0]
    relayed = [e for e in FIRST if e[0] != 0]

    def queue(n):
        for w in eager:
            if n < CHUNKS:
                chunk(first_of[w], n).start()
            elif n < 2 * CHUNKS:
                chunk(second_of[w], n - CHUNKS).start()

    def got(slot, n):
        chunk((0, slot, 0), n).wait_recv()
        if slot in SHARED:
            across(slot, n).start()

    def row_ids(slot):
        wide = jnp.broadcast_to(cid[slot, core], (128, rows))
        rid[slot] = wide.T

    def compare(columns, which, begin, count, own=False):
        a = jnp.concatenate([buf[i, core, pl.ds(begin, count)] for i in which], axis=0)
        b = jnp.concatenate([buf[columns, 0], buf[columns, 1]], axis=0)
        s = lax.dot_general(a, b, (((1,), (1,)), ((), ())), preferred_element_type=jnp.float32)
        left = jnp.concatenate([rid[i, pl.ds(begin, count)] for i in which], axis=0)
        mask = jnp.concatenate([left] * (2 * rows // 128), axis=1) == jnp.concatenate(
            [cid[columns, 0], cid[columns, 1]], axis=1
        )
        if own:
            at = lax.broadcasted_iota(jnp.int32, s.shape, 0) + core * rows
            mask = mask & (at != lax.broadcasted_iota(jnp.int32, s.shape, 1))
        s = jnp.where(mask, s, -1.0)
        best = s[:, :128]
        for q in range(1, 2 * rows // 128):
            best = jnp.maximum(best, s[:, 128 * q : 128 * q + 128])
        for n, i in enumerate(which):
            rowacc[i, pl.ds(begin, count)] = jnp.maximum(
                rowacc[i, pl.ds(begin, count)], best[n * count : (n + 1) * count]
            )
        if not own:
            total = jnp.max(s.reshape(s.shape[0] // 8, 8, s.shape[1]), axis=0)
            colacc[columns] = jnp.maximum(colacc[columns], total)

    ids_across().start()
    for n in range(AHEAD):
        queue(n)
    for n in range(CHUNKS):
        across(0, n).start()
    ids_across().wait()
    for e in FIRST:
        if e[0] == 0:
            ids(e).start()
    for e in FIRST:
        if e[0] == 0:
            ids((0, e[1], 0)).wait_recv()
            for f in FIRST + SECOND:
                if f[0] == e[1]:
                    ids(f).start()
    row_ids(0)
    for e in FIRST:
        if e[0] == 0:
            row_ids(e[1])

    work = {}
    work[0] = [lambda: compare(0, (0,), 0, rows, own=True)]
    for t, (j, which) in enumerate(EARLY):
        work[CHUNKS + 1 + t] = [functools.partial(compare, j, which, 0, rows)]
    half = rows // 2
    for t, (j, which) in enumerate(LATE):
        work.setdefault(CHUNKS + 5 + t // 2, []).append(functools.partial(compare, j, which, 0, half))

    for step in range(2 * CHUNKS + 1):
        queue(step + AHEAD)
        if step < CHUNKS:
            for e in FIRST:
                if e[0] == 0:
                    got(e[1], step)
                    for f in relayed:
                        if f[0] == e[1]:
                            chunk(f, step).start()
        if 1 <= step <= CHUNKS:
            for f in relayed:
                got(f[1], step - 1)
        if CHUNKS <= step < 2 * CHUNKS:
            for w in range(6):
                if w not in eager:
                    chunk(second_of[w], step - CHUNKS).start()
            for w in eager:
                got(second_of[w][1], step - CHUNKS)
        if step > CHUNKS:
            for w in range(6):
                if w not in eager:
                    got(second_of[w][1], step - CHUNKS - 1)
        if step == 0:
            whole(0).wait_recv()
        if step == 1:
            for f in relayed:
                ids((0, f[1], 0)).wait_recv()
                for e in SECOND:
                    if e[0] == f[1]:
                        ids(e).start()
                row_ids(f[1])
        if step == 2:
            for e in SECOND:
                ids((0, e[1], 0)).wait_recv()
                row_ids(e[1])
        if step == CHUNKS + 1:
            for slot in SHARED[1:-1]:
                whole(slot).wait_recv()
        for job in work.get(step, ()):
            job()
    for j, which in LATE:
        compare(j, which, half, rows - half)
    whole(SHARED[-1]).wait_recv()
    for j, which in LAST:
        compare(j, which, 0, rows)

    def result(slot, which):
        return remote(outb.at[slot, which], inb.at[slot, core], res_sent, res_in, device(owner(slot), which))

    def result_pair():
        return remote(outb.at[0, 1 - core], inb.at[0, core], res_pair_sent, res_pair_in, sibling)

    for slot in range(K):
        down = jnp.max(colacc[slot], axis=0, keepdims=True)
        outb[slot, 0] = down[:, :rows]
        outb[slot, 1] = down[:, rows:]
        along = jnp.max(rowacc[slot].T, axis=0, keepdims=True)
        outb[slot, core] = jnp.maximum(outb[slot, core], along)
        if slot == 0:
            result_pair().start()
        else:
            for which in range(2):
                result(slot, which).start()
    result_pair().wait()
    everything = pltpu.make_async_remote_copy(
        src_ref=outb.at[pl.ds(1, K - 1)], dst_ref=inb.at[pl.ds(1, K - 1)], send_sem=res_sent, recv_sem=res_in,
        device_id=sibling, device_id_type=MESH,
    )
    everything.wait_recv()
    best = jnp.maximum(outb[0, core], inb[0, 1 - core])
    best = jnp.maximum(best, jnp.max(jnp.max(inb[pl.ds(1, K - 1)], axis=0), axis=0))
    out_ref[...] = jnp.maximum(best, -1.0)

    everything.wait_send()
    for src, dst, which in FIRST + SECOND:
        ids((src, dst, which)).wait_send()
        remote(buf.at[src, core], buf.at[dst, core], sent.at[dst], arrive.at[dst, 0], links[which]).wait_send()
    for slot in SHARED:
        whole(slot).wait_send()


def per_device(embeddings, cluster):
    rows, width = embeddings.shape
    dma = pltpu.SemaphoreType.DMA
    best = pl.pallas_call(
        kernel,
        out_shape=jax.ShapeDtypeStruct((1, rows), jnp.float32),
        in_specs=[pl.BlockSpec(memory_space=pltpu.VMEM)] * 2,
        out_specs=pl.BlockSpec(memory_space=pltpu.VMEM),
        scratch_shapes=[
            pltpu.VMEM((K, 2, rows, width), jnp.bfloat16),
            pltpu.VMEM((K, 2, 1, rows), jnp.int32),
            pltpu.VMEM((K, rows, 128), jnp.int32),
            pltpu.VMEM((K, rows, 128), jnp.float32),
            pltpu.VMEM((K, 8, 2 * rows), jnp.float32),
            pltpu.VMEM((K, 2, 1, rows), jnp.float32),
            pltpu.VMEM((K, 2, 1, rows), jnp.float32),
            dma((K, CHUNKS)), dma((K,)), dma((K,)), dma, dma((K,)), dma((K,)), dma((K,)), dma,
            dma, dma, dma, dma,
        ],
        compiler_params=pltpu.CompilerParams(
            collective_id=0, has_side_effects=True, vmem_limit_bytes=56 * 2**20
        ),
    )(embeddings, cluster.reshape(1, rows))
    return best.reshape(rows)


def solution(mesh):
    placed = (P(("group", "tile"), None), P(("group", "tile")))
    return jax.shard_map(
        per_device, mesh=mesh, in_specs=placed, out_specs=P(("group", "tile")), check_vma=False
    )
```

```python
import functools

import jax
import jax.numpy as jnp
from jax import lax
from jax.experimental import pallas as pl
from jax.experimental.pallas import tpu as pltpu
from jax.sharding import PartitionSpec as P

EPS = 1e-06
MESH = pl.DeviceIdType.MESH

TWIST = ((0, 1, 0), (0, 0, 0), (1, 0, 0))
SLOTS = (
    (0, 0, 0), (1, 0, 0), (0, 1, 0), (0, 0, 1), (3, 0, 1), (1, 3, 0), (0, 1, 3),
    (2, 0, 0), (2, 3, 0), (0, 2, 0), (0, 3, 1), (1, 0, 3), (0, 1, 2),
)
FIRST = ((0, 1, 0), (0, 2, 2), (0, 3, 4), (3, 4, 1), (1, 5, 3), (2, 6, 5))
SECOND = ((1, 7, 0), (5, 8, 1), (2, 9, 2), (3, 10, 3), (1, 11, 4), (6, 12, 5))
EARLY = ((0, (1, 2, 3, 4, 5)), (4, (1, 2, 3, 5)), (5, (1, 2, 3, 6)), (6, (1, 3, 4, 0)))
LATE = ((0, (9, 11, 7)), (2, (12, 8)), (3, (8, 9)), (4, (9, 11, 10, 12)), (5, (12, 11)), (6, (10, 8, 11)))
LAST = ((12, (7, 8)),)
SHARED = (0, 2, 3, 4, 5, 6, 12)

K = len(SLOTS)
CHUNKS = 8
AHEAD = 4
LAG = 3


def chi(axis, parities):
    return sum(t * p for t, p in zip(TWIST[axis], parities)) % 2


def kernel(x_ref, cluster_ref, out_ref, buf, cid, rid, rowacc, colacc, outb, inb,
           arrive, shared, ids_in, ids_pair, sent, sent_pair, ids_sent, ids_pair_sent,
           res_in, res_pair_in, res_sent, res_pair_sent):
    rows = x_ref.shape[0]
    part = rows // CHUNKS
    group, tile = lax.axis_index("group"), lax.axis_index("tile")
    core = lax.rem(group, 2)
    here = (group // 2, tile // 4, lax.rem(tile, 4))
    odd = [lax.rem(h, 2) for h in here]
    sign = [1 - 2 * lax.rem(sum(t * o for t, o in zip(TWIST[a], odd)) + 0 * odd[0], 2) for a in range(3)]

    def device(chip, which):
        return (chip[0] * 2 + which, chip[1] * 4 + chip[2])

    def link(which):
        axis, step = which // 2, 1 - 2 * (which % 2)
        chip = list(here)
        chip[axis] = lax.rem(here[axis] + sign[axis] * step + 4, 4)
        return chip

    def owner(slot):
        s = SLOTS[slot]
        flip = [1 - 2 * chi(a, [v % 2 for v in s]) for a in range(3)]
        return [lax.rem(here[a] - sign[a] * (flip[a] * s[a]) + 8, 4) for a in range(3)]

    sibling = device(here, 1 - core)
    links = [device(link(w), core) for w in range(6)]

    barrier = pltpu.get_barrier_semaphore()
    partners = links + [sibling]
    for partner in partners:
        pl.semaphore_signal(barrier, inc=1, device_id=partner, device_id_type=MESH)

    e32 = x_ref[...].astype(jnp.float32)
    normed = e32 * lax.rsqrt(jnp.sum(e32 * e32, axis=1, keepdims=True) + EPS)
    buf[0, core] = normed.astype(jnp.bfloat16)
    cid[0, core] = cluster_ref[...]
    rowacc[...] = jnp.full(rowacc.shape, -1.0, jnp.float32)
    colacc[...] = jnp.full(colacc.shape, -1.0, jnp.float32)

    pl.semaphore_wait(barrier, len(partners))

    def remote(src, dst, send, recv, to):
        return pltpu.make_async_remote_copy(
            src_ref=src, dst_ref=dst, send_sem=send, recv_sem=recv, device_id=to, device_id_type=MESH
        )

    def chunk(edge, n):
        src, dst, which = edge
        piece = pl.ds(n * part, part)
        return remote(buf.at[src, core, piece], buf.at[dst, core, piece], sent.at[dst], arrive.at[dst, n], links[which])

    def across(slot, n):
        piece = pl.ds(n * part, part)
        return remote(buf.at[slot, core, piece], buf.at[slot, core, piece], sent_pair.at[slot], shared.at[slot], sibling)

    def whole(slot):
        return remote(buf.at[slot, core], buf.at[slot, core], sent_pair.at[slot], shared.at[slot], sibling)

    def ids_across(slot):
        return remote(cid.at[slot, core], cid.at[slot, core], ids_pair_sent.at[slot], ids_pair.at[slot], sibling)

    def ids(edge):
        src, dst, which = edge
        return remote(cid.at[src, core], cid.at[dst, core], ids_sent.at[dst], ids_in.at[dst], links[which])

    def got_ids(slot):
        ids((0, slot, 0)).wait_recv()
        for e in FIRST + SECOND:
            if e[0] == slot:
                ids(e).start()
        if slot in SHARED:
            ids_across(slot).start()
        row_ids(slot)

    first_of = {e[2]: e for e in FIRST}
    second_of = {e[2]: e for e in SECOND}
    eager = [w for w in range(6) if first_of[w][0] == 0]
    relayed = [e for e in FIRST if e[0] != 0]

    def queue(n):
        for w in eager:
            if n < CHUNKS:
                chunk(first_of[w], n).start()
            elif n < 2 * CHUNKS:
                chunk(second_of[w], n - CHUNKS).start()

    def got(slot, n):
        chunk((0, slot, 0), n).wait_recv()
        if slot in SHARED:
            across(slot, n).start()

    def row_ids(slot):
        wide = jnp.broadcast_to(cid[slot, core], (128, rows))
        rid[slot] = wide.T

    def compare(columns, which, begin, count, own=False):
        a = jnp.concatenate([buf[i, core, pl.ds(begin, count)] for i in which], axis=0)
        b = jnp.concatenate([buf[columns, 0], buf[columns, 1]], axis=0)
        s = lax.dot_general(a, b, (((1,), (1,)), ((), ())), preferred_element_type=jnp.float32)
        left = jnp.concatenate([rid[i, pl.ds(begin, count)] for i in which], axis=0)
        mask = jnp.concatenate([left] * (2 * rows // 128), axis=1) == jnp.concatenate(
            [cid[columns, 0], cid[columns, 1]], axis=1
        )
        if own:
            at = lax.broadcasted_iota(jnp.int32, s.shape, 0) + core * rows
            mask = mask & (at != lax.broadcasted_iota(jnp.int32, s.shape, 1))
        s = jnp.where(mask, s, -1.0)
        best = s[:, :128]
        for q in range(1, 2 * rows // 128):
            best = jnp.maximum(best, s[:, 128 * q : 128 * q + 128])
        for n, i in enumerate(which):
            rowacc[i, pl.ds(begin, count)] = jnp.maximum(
                rowacc[i, pl.ds(begin, count)], best[n * count : (n + 1) * count]
            )
        if not own:
            total = jnp.max(s.reshape(s.shape[0] // 8, 8, s.shape[1]), axis=0)
            colacc[columns] = jnp.maximum(colacc[columns], total)

    for e in FIRST + SECOND:
        if e[0] == 0:
            ids(e).start()
    for n in range(AHEAD):
        queue(n)
    ids_across(0).start()
    for n in range(CHUNKS):
        across(0, n).start()
    row_ids(0)

    work = {}
    work[1] = [lambda: compare(0, (0,), 0, rows, own=True)]
    for t, (j, which) in enumerate(EARLY):
        work[CHUNKS + LAG + t] = [functools.partial(compare, j, which, 0, rows)]
    half = rows // 2
    for t, (j, which) in enumerate(LATE):
        work.setdefault(CHUNKS + LAG + 4 + t // 2, []).append(functools.partial(compare, j, which, 0, half))

    for step in range(2 * CHUNKS + LAG):
        queue(step + AHEAD)
        if step < CHUNKS:
            for e in FIRST:
                if e[0] == 0:
                    got(e[1], step)
                    for f in relayed:
                        if f[0] == e[1]:
                            chunk(f, step).start()
        if LAG <= step < CHUNKS + LAG:
            for f in relayed:
                got(f[1], step - LAG)
        if CHUNKS <= step < 2 * CHUNKS:
            for w in range(6):
                if w not in eager:
                    chunk(second_of[w], step - CHUNKS).start()
            for w in eager:
                got(second_of[w][1], step - CHUNKS)
        if step >= CHUNKS + LAG:
            for w in range(6):
                if w not in eager:
                    got(second_of[w][1], step - CHUNKS - LAG)
        if step == 0:
            for e in FIRST:
                if e[0] == 0:
                    got_ids(e[1])
        if step == 1:
            ids_across(0).wait_recv()
            whole(0).wait_recv()
        if step == LAG:
            for f in relayed:
                got_ids(f[1])
        if step == CHUNKS:
            for e in SECOND:
                got_ids(e[1])
        if step == CHUNKS + LAG:
            for slot in SHARED[1:-1]:
                ids_across(slot).wait_recv()
                whole(slot).wait_recv()
        for job in work.get(step, ()):
            job()
    for j, which in LATE:
        compare(j, which, half, rows - half)
    ids_across(SHARED[-1]).wait_recv()
    whole(SHARED[-1]).wait_recv()
    for j, which in LAST:
        compare(j, which, 0, rows)

    def result(slot, which):
        return remote(outb.at[slot, which], inb.at[slot, core], res_sent, res_in, device(owner(slot), which))

    def result_pair():
        return remote(outb.at[0, 1 - core], inb.at[0, core], res_pair_sent, res_pair_in, sibling)

    for slot in range(K):
        down = jnp.max(colacc[slot], axis=0, keepdims=True)
        outb[slot, 0] = down[:, :rows]
        outb[slot, 1] = down[:, rows:]
        along = jnp.max(rowacc[slot].T, axis=0, keepdims=True)
        outb[slot, core] = jnp.maximum(outb[slot, core], along)
        if slot == 0:
            result_pair().start()
        else:
            for which in range(2):
                result(slot, which).start()
    result_pair().wait()
    everything = pltpu.make_async_remote_copy(
        src_ref=outb.at[pl.ds(1, K - 1)], dst_ref=inb.at[pl.ds(1, K - 1)], send_sem=res_sent, recv_sem=res_in,
        device_id=sibling, device_id_type=MESH,
    )
    everything.wait_recv()
    best = jnp.maximum(outb[0, core], inb[0, 1 - core])
    best = jnp.maximum(best, jnp.max(jnp.max(inb[pl.ds(1, K - 1)], axis=0), axis=0))
    out_ref[...] = jnp.maximum(best, -1.0)[0]

    everything.wait_send()
    for src, dst, which in FIRST + SECOND:
        ids((src, dst, which)).wait_send()
        remote(buf.at[src, core], buf.at[dst, core], sent.at[dst], arrive.at[dst, 0], links[which]).wait_send()
    for slot in SHARED:
        ids_across(slot).wait_send()
        whole(slot).wait_send()


def per_device(embeddings, cluster):
    rows, width = embeddings.shape
    dma = pltpu.SemaphoreType.DMA
    return pl.pallas_call(
        kernel,
        out_shape=jax.ShapeDtypeStruct((rows,), jnp.float32),
        in_specs=[pl.BlockSpec(memory_space=pltpu.VMEM)] * 2,
        out_specs=pl.BlockSpec(memory_space=pltpu.VMEM),
        scratch_shapes=[
            pltpu.VMEM((K, 2, rows, width), jnp.bfloat16),
            pltpu.VMEM((K, 2, 1, rows), jnp.int32),
            pltpu.VMEM((K, rows, 128), jnp.int32),
            pltpu.VMEM((K, rows, 128), jnp.float32),
            pltpu.VMEM((K, 8, 2 * rows), jnp.float32),
            pltpu.VMEM((K, 2, 1, rows), jnp.float32),
            pltpu.VMEM((K, 2, 1, rows), jnp.float32),
            dma((K, CHUNKS)), dma((K,)), dma((K,)), dma((K,)), dma((K,)), dma((K,)), dma((K,)), dma((K,)),
            dma, dma, dma, dma,
        ],
        compiler_params=pltpu.CompilerParams(
            collective_id=0, has_side_effects=True, vmem_limit_bytes=56 * 2**20
        ),
    )(embeddings, cluster.reshape(1, rows))


def solution(mesh):
    placed = (P(("group", "tile"), None), P(("group", "tile")))
    return jax.shard_map(
        per_device, mesh=mesh, in_specs=placed, out_specs=P(("group", "tile")), check_vma=False
    )
```

```python
import functools

import jax
import jax.numpy as jnp
from jax import lax
from jax.experimental import pallas as pl
from jax.experimental.pallas import tpu as pltpu
from jax.sharding import PartitionSpec as P

EPS = 1e-06
MESH = pl.DeviceIdType.MESH

SLOTS = (
    (0, 0, 0), (1, 0, 0), (3, 0, 0), (0, 1, 0), (0, 0, 1), (1, 3, 0), (3, 0, 3),
    (1, 1, 0), (3, 1, 0), (0, 2, 0), (0, 0, 2), (1, 2, 0), (3, 0, 2),
)
FIRST = ((0, 1, 0), (0, 2, 1), (0, 3, 2), (0, 4, 4), (1, 5, 3), (2, 6, 5))
SECOND = ((3, 7, 0), (3, 8, 1), (3, 9, 2), (4, 10, 4), (5, 11, 3), (6, 12, 5))
NEAR = ((4, (0, 2, 3)), (3, (0, 2, 1)), (1, (0, 2, 4)))
RELAYED = ((5, (3, 4, 2)), (6, (4, 3, 1, 5)))
FAR = ((0, (10, 9)), (4, (9, 7, 8)), (3, (10,)), (5, (10, 8)), (6, (8, 9, 7)))
LAST = ((4, (11,)), (6, (11,)))
LAST_FULL = ((10, (9, 7, 11)), (7, (12,)))
LAST_EITHER = ((1, 11), (12,))
ARRIVING = ((1, 2, 3, 4), (5, 6), (7, 8, 9, 10, 11, 12))
TOGETHER = ((0,), (1, 3, 4), (5, 6), (7, 10, 11))
SHARED = (0, 1, 3, 4, 5, 6, 7, 10, 11)

K = len(SLOTS)
BOUNDS = (0, 32, 64, 96, 128, 160, 192, 224, 256)
CHUNKS = len(BOUNDS) - 1
HALFWAY = 4
AHEAD = 3


def kernel(x_ref, cluster_ref, out_ref, buf, cid, rid, rowacc, colacc, outb, inb,
           arrive, shared, ids_in, ids_pair, sent, sent_pair, ids_sent, ids_pair_sent,
           res_in, res_pair_in, res_sent, res_pair_sent):
    rows = x_ref.shape[0]
    half = rows // 2
    group, tile = lax.axis_index("group"), lax.axis_index("tile")
    core = lax.rem(group, 2)
    here = (group // 2, tile // 4, lax.rem(tile, 4))
    def device(chip, which):
        return (chip[0] * 2 + which, chip[1] * 4 + chip[2])

    def link(which):
        axis, step = which // 2, 1 - 2 * (which % 2)
        chip = list(here)
        chip[axis] = lax.rem(here[axis] + step + 4, 4)
        return chip

    def owner(slot):
        return [lax.rem(h - s + 4, 4) for h, s in zip(here, SLOTS[slot])]

    sibling = device(here, 1 - core)
    links = [device(link(w), core) for w in range(6)]

    barrier = pltpu.get_barrier_semaphore()
    partners = links + [sibling]
    for partner in partners:
        pl.semaphore_signal(barrier, inc=1, device_id=partner, device_id_type=MESH)

    e32 = x_ref[...].astype(jnp.float32)
    normed = e32 * lax.rsqrt(jnp.sum(e32 * e32, axis=1, keepdims=True) + EPS)
    buf[0, core] = normed.astype(jnp.bfloat16)
    cid[0, core] = cluster_ref[...]
    rowacc[...] = jnp.full(rowacc.shape, -1.0, jnp.float32)
    colacc[...] = jnp.full(colacc.shape, -1.0, jnp.float32)

    pl.semaphore_wait(barrier, len(partners))

    def remote(src, dst, send, recv, to):
        return pltpu.make_async_remote_copy(
            src_ref=src, dst_ref=dst, send_sem=send, recv_sem=recv, device_id=to, device_id_type=MESH
        )

    def piece(begin, end):
        return pl.ds(begin, end - begin)

    def move(edge, rows_of, sem):
        src, dst, which = edge
        return remote(buf.at[src, core, rows_of], buf.at[dst, core, rows_of], sent, sem, links[which])

    def chunk(edge, n):
        dst = edge[1]
        sem = arrive.at[(dst - 1) * CHUNKS + n if dst in (1, 2) else 2 * CHUNKS + 2 * (dst - 3) + n // HALFWAY]
        return move(edge, piece(BOUNDS[n], BOUNDS[n + 1]), sem)

    def part(edge, h):
        return move(edge, piece(h * half, (h + 1) * half), arrive.at[2 * CHUNKS + 2 * (edge[1] - 3) + h])

    def got(slot, h):
        part((0, slot, 0), h).wait_recv()

    def across(slot, h):
        rows_of = piece(h * half, (h + 1) * half)
        return remote(buf.at[slot, core, rows_of], buf.at[slot, core, rows_of], sent_pair, shared.at[slot], sibling)

    def whole(slot):
        return remote(buf.at[slot, core], buf.at[slot, core], sent_pair, shared.at[slot], sibling)

    def whole_shared(*slots):
        some = pl.ds(0, len(slots))
        remote(cid.at[some, core], cid.at[some, core], ids_pair_sent, ids_pair.at[slots[0]], sibling).wait_recv()
        for slot in slots:
            whole(slot).wait_recv()

    def ids_across(slot):
        group = next(g for g in TOGETHER if slot in g)[0]
        return remote(cid.at[slot, core], cid.at[slot, core], ids_pair_sent, ids_pair.at[group], sibling)

    def ids(edge):
        src, dst, which = edge
        group = next(g for g in ARRIVING if dst in g)[0]
        return remote(cid.at[src, core], cid.at[dst, core], ids_sent, ids_in.at[group], links[which])

    def got_ids(*slots):
        some = pl.ds(slots[0], len(slots))
        remote(cid.at[some, core], cid.at[some, core], ids_sent, ids_in.at[slots[0]], sibling).wait_recv()
        for slot in slots:
            for e in FIRST + SECOND:
                if e[0] == slot:
                    ids(e).start()
            if slot in SHARED:
                ids_across(slot).start()
        for slot in slots:
            row_ids(slot)

    edge_to = {e[1]: e for e in FIRST + SECOND}

    def row_ids(slot):
        wide = jnp.broadcast_to(cid[slot, core], (128, rows))
        rid[slot] = wide.T

    def compare(columns, pieces, own=False):
        a = jnp.concatenate([buf[i, core, pl.ds(begin, count)] for i, begin, count in pieces], axis=0)
        b = jnp.concatenate([buf[columns, 0], buf[columns, 1]], axis=0)
        s = lax.dot_general(a, b, (((1,), (1,)), ((), ())), preferred_element_type=jnp.float32)
        left = jnp.concatenate([rid[i, pl.ds(begin, count)] for i, begin, count in pieces], axis=0)
        mask = jnp.concatenate([left] * (2 * rows // 128), axis=1) == jnp.concatenate(
            [cid[columns, 0], cid[columns, 1]], axis=1
        )
        if own:
            at = lax.broadcasted_iota(jnp.int32, s.shape, 0) + core * rows
            mask = mask & (at != lax.broadcasted_iota(jnp.int32, s.shape, 1))
        s = jnp.where(mask, s, -1.0)
        best = s[:, :128]
        for q in range(1, 2 * rows // 128):
            best = jnp.maximum(best, s[:, 128 * q : 128 * q + 128])
        row = 0
        for i, begin, count in pieces:
            rowacc[i, pl.ds(begin, count)] = jnp.maximum(rowacc[i, pl.ds(begin, count)], best[row : row + count])
            row += count
        if not own:
            total = jnp.max(s.reshape(s.shape[0] // 8, 8, s.shape[1]), axis=0)
            colacc[columns] = jnp.maximum(colacc[columns], total)

    def full(which):
        return [(i, 0, rows) for i in which]

    def halves(which, h):
        return [(i, h * half, half) for i in which]

    for dst in (1, 2, 3, 4):
        ids(edge_to[dst]).start()
    for n in range(AHEAD):
        for dst in (1, 2):
            chunk(edge_to[dst], n).start()
        if n == 0:
            for dst in (3, 4):
                part(edge_to[dst], 0).start()
    ids_across(0).start()
    for h in range(2):
        across(0, h).start()
    row_ids(0)

    for n in range(CHUNKS):
        for dst in (1, 2):
            if n + AHEAD < CHUNKS:
                chunk(edge_to[dst], n + AHEAD).start()
        if n + AHEAD == CHUNKS:
            for dst in (7, 8):
                part(edge_to[dst], 0).start()
        for src, dst in ((1, 5), (2, 6)):
            chunk(edge_to[src], n).wait_recv()
            chunk(edge_to[dst], n).start()
        if n == 0:
            got_ids(1, 2, 3, 4)
        if n == 1:
            for dst in (3, 4):
                part(edge_to[dst], 1).start()
            whole_shared(0)
            compare(0, full((0,)), own=True)
        if n == HALFWAY:
            for dst in (3, 4):
                got(dst, 0)
            for dst in (9, 10):
                part(edge_to[dst], 0).start()
            for dst in (1, 3, 4):
                across(dst, 0).start()
            got_ids(5, 6)
    for dst in (5, 6):
        got(dst, 0)
    for dst in (11, 12):
        part(edge_to[dst], 0).start()
    for dst in (3, 4):
        got(dst, 1)
    for dst in (7, 8, 9, 10):
        part(edge_to[dst], 1).start()
    for dst in (1, 3, 4):
        across(dst, 1).start()
    for dst in (5, 6):
        across(dst, 0).start()
    whole_shared(1, 3, 4)
    compare(NEAR[0][0], full(NEAR[0][1]))
    for dst in (5, 6):
        got(dst, 1)
    for dst in (11, 12):
        part(edge_to[dst], 1).start()
    for dst in (5, 6):
        across(dst, 1).start()
    got_ids(7, 8, 9, 10, 11, 12)
    for j, which in NEAR[1:]:
        compare(j, full(which))
    whole_shared(5, 6)
    for j, which in RELAYED:
        compare(j, full(which))

    for h in range(2):
        for dst in (7, 8, 9, 10):
            got(dst, h)
        for dst in (7, 10):
            across(dst, h).start()
        for j, which in FAR:
            compare(j, halves(which, h))
        for dst in (11, 12):
            got(dst, h)
        across(11, h).start()
        for j, which in LAST:
            compare(j, halves(which, h))
    whole_shared(7, 10, 11)
    for j, which in LAST_FULL:
        compare(j, full(which))
    either, which = LAST_EITHER
    compare(jnp.where(here[0] // 2 == 0, *either), full(which))

    def result(slot, which):
        return remote(outb.at[slot, which], inb.at[slot, core], res_sent, res_in, device(owner(slot), which))

    def result_pair():
        return remote(outb.at[0, 1 - core], inb.at[0, core], res_pair_sent, res_pair_in, sibling)

    for slot in range(K):
        down = jnp.max(colacc[slot], axis=0, keepdims=True)
        outb[slot, 0] = down[:, :rows]
        outb[slot, 1] = down[:, rows:]
        along = jnp.max(rowacc[slot].T, axis=0, keepdims=True)
        outb[slot, core] = jnp.maximum(outb[slot, core], along)
        if slot == 0:
            result_pair().start()
        else:
            for which in range(2):
                result(slot, which).start()
    result_pair().wait()
    everything = pltpu.make_async_remote_copy(
        src_ref=outb.at[pl.ds(1, K - 1)], dst_ref=inb.at[pl.ds(1, K - 1)], send_sem=res_sent, recv_sem=res_in,
        device_id=sibling, device_id_type=MESH,
    )
    everything.wait_recv()
    best = jnp.maximum(outb[0, core], inb[0, 1 - core])
    best = jnp.maximum(best, jnp.max(jnp.max(inb[pl.ds(1, K - 1)], axis=0), axis=0))
    out_ref[...] = jnp.maximum(best, -1.0)[0]

    everything.wait_send()
    every, across_all = pl.ds(0, len(FIRST + SECOND)), pl.ds(0, len(SHARED))
    remote(cid.at[every, core], cid.at[every, core], ids_sent, ids_in.at[0], sibling).wait_send()
    remote(buf.at[every, core], buf.at[every, core], sent, arrive.at[0], sibling).wait_send()
    remote(cid.at[across_all, core], cid.at[across_all, core], ids_pair_sent, ids_pair.at[0], sibling).wait_send()
    remote(buf.at[across_all, core], buf.at[across_all, core], sent_pair, shared.at[0], sibling).wait_send()


def per_device(embeddings, cluster):
    rows, width = embeddings.shape
    dma = pltpu.SemaphoreType.DMA
    return pl.pallas_call(
        kernel,
        out_shape=jax.ShapeDtypeStruct((rows,), jnp.float32),
        in_specs=[pl.BlockSpec(memory_space=pltpu.VMEM)] * 2,
        out_specs=pl.BlockSpec(memory_space=pltpu.VMEM),
        scratch_shapes=[
            pltpu.VMEM((K, 2, rows, width), jnp.bfloat16),
            pltpu.VMEM((K, 2, 1, rows), jnp.int32),
            pltpu.VMEM((K, rows, 128), jnp.int32),
            pltpu.VMEM((K, rows, 128), jnp.float32),
            pltpu.VMEM((K, 8, 2 * rows), jnp.float32),
            pltpu.VMEM((K, 2, 1, rows), jnp.float32),
            pltpu.VMEM((K, 2, 1, rows), jnp.float32),
            dma((2 * CHUNKS + 2 * (K - 3),)), dma((K,)), dma((K,)), dma((K,)), dma, dma, dma, dma,
            dma, dma, dma, dma,
        ],
        compiler_params=pltpu.CompilerParams(
            collective_id=0, has_side_effects=True, vmem_limit_bytes=56 * 2**20
        ),
    )(embeddings, cluster.reshape(1, rows))


def solution(mesh):
    placed = (P(("group", "tile"), None), P(("group", "tile")))
    return jax.shard_map(
        per_device, mesh=mesh, in_specs=placed, out_specs=P(("group", "tile")), check_vma=False
    )
```

```python
import functools

import jax
import jax.numpy as jnp
from jax import lax
from jax.experimental import pallas as pl
from jax.experimental.pallas import tpu as pltpu
from jax.sharding import PartitionSpec as P

EPS = 1e-06
MESH = pl.DeviceIdType.MESH

SLOTS = (
    (0, 0, 0), (1, 0, 0), (3, 0, 0), (0, 1, 0), (0, 0, 1), (1, 3, 0), (3, 0, 3),
    (1, 1, 0), (3, 1, 0), (0, 2, 0), (0, 0, 2), (1, 2, 0), (3, 0, 2),
)
FIRST = ((0, 1, 0), (0, 2, 1), (0, 3, 2), (0, 4, 4), (1, 5, 3), (2, 6, 5))
SECOND = ((3, 7, 0), (3, 8, 1), (3, 9, 2), (4, 10, 4), (5, 11, 3), (6, 12, 5))
NEAR = ((4, (0, 2, 3)), (3, (0, 2, 1)), (1, (0, 2, 4)))
RELAYED = ((5, (3, 4, 2)), (6, (4, 3, 1, 5)))
FAR = ((0, (10, 9)), (4, (9, 7, 8)), (3, (10,)), (5, (10, 8)), (6, (8, 9, 7)))
LAST = ((4, (11,)), (6, (11,)))
LAST_FULL = ((10, (9, 7, 11)), (7, (12,)))
LAST_EITHER = ((1, 11), (12,))
ARRIVING = ((1, 2, 3, 4), (5, 6), (7, 8, 9, 10, 11, 12))
TOGETHER = ((0,), (1, 3, 4), (5, 6), (7, 10, 11))
DONE_NEAR, DONE_FAR, DONE_LAST, DONE_FULL, DONE = (2,), (0, 3, 5, 8), (4, 6), (7, 9, 10), (1, 11, 12)
SHARED = (0, 1, 3, 4, 5, 6, 7, 10, 11)

K = len(SLOTS)
BOUNDS = tuple(range(0, 257, 16))
CHUNKS = len(BOUNDS) - 1
HALFWAY = 8
AHEAD = 7


def kernel(x_hbm, cluster_hbm, out_ref, x_ref, cluster_ref, buf, cid, rid, rowacc, colacc, outb, inb,
           arrive, shared, ids_in, ids_pair, sent, sent_pair, ids_sent, ids_pair_sent,
           res_in, res_pair_in, res_sent, res_pair_sent, loaded, loaded_ids):
    rows = x_ref.shape[0]
    half = rows // 2
    group, tile = lax.axis_index("group"), lax.axis_index("tile")
    core = lax.rem(group, 2)
    here = (group // 2, tile // 4, lax.rem(tile, 4))
    def device(chip, which):
        return (chip[0] * 2 + which, chip[1] * 4 + chip[2])

    def link(which):
        axis, step = which // 2, 1 - 2 * (which % 2)
        chip = list(here)
        chip[axis] = lax.rem(here[axis] + step + 4, 4)
        return chip

    def owner(slot):
        return [lax.rem(h - s + 4, 4) for h, s in zip(here, SLOTS[slot])]

    sibling = device(here, 1 - core)
    links = [device(link(w), core) for w in range(6)]

    barrier = pltpu.get_barrier_semaphore()
    partners = links + [sibling]
    for partner in partners:
        pl.semaphore_signal(barrier, inc=1, device_id=partner, device_id_type=MESH)

    quarter = rows // 4

    def load(q):
        rows_of = pl.ds(q * quarter, quarter)
        return pltpu.make_async_copy(x_hbm.at[rows_of], x_ref.at[rows_of], loaded.at[q])

    load_ids = pltpu.make_async_copy(cluster_hbm, cluster_ref, loaded_ids)
    load(0).start()
    load_ids.start()
    for q in range(1, 4):
        load(q).start()

    def normalise(q):
        rows_of = pl.ds(q * quarter, quarter)
        load(q).wait()
        e32 = x_ref[rows_of].astype(jnp.float32)
        normed = e32 * lax.rsqrt(jnp.sum(e32 * e32, axis=1, keepdims=True) + EPS)
        buf[0, core, rows_of] = normed.astype(jnp.bfloat16)

    def remote(src, dst, send, recv, to):
        return pltpu.make_async_remote_copy(
            src_ref=src, dst_ref=dst, send_sem=send, recv_sem=recv, device_id=to, device_id_type=MESH
        )

    def piece(begin, end):
        return pl.ds(begin, end - begin)

    def move(edge, rows_of, sem):
        src, dst, which = edge
        return remote(buf.at[src, core, rows_of], buf.at[dst, core, rows_of], sent, sem, links[which])

    def chunk(edge, n):
        dst = edge[1]
        sem = arrive.at[(dst - 1) * CHUNKS + n if dst in (1, 2) else 2 * CHUNKS + 2 * (dst - 3) + n // HALFWAY]
        return move(edge, piece(BOUNDS[n], BOUNDS[n + 1]), sem)

    def part(edge, h):
        return move(edge, piece(h * half, (h + 1) * half), arrive.at[2 * CHUNKS + 2 * (edge[1] - 3) + h])

    def got(slot, h):
        part((0, slot, 0), h).wait_recv()

    def across(slot, h):
        rows_of = piece(h * half, (h + 1) * half)
        return remote(buf.at[slot, core, rows_of], buf.at[slot, core, rows_of], sent_pair, shared.at[slot], sibling)

    def whole(slot):
        return remote(buf.at[slot, core], buf.at[slot, core], sent_pair, shared.at[slot], sibling)

    def paired_ids(*slots):
        some = pl.ds(0, len(slots))
        remote(cid.at[some, core], cid.at[some, core], ids_pair_sent, ids_pair.at[slots[0]], sibling).wait_recv()

    def paired(*slots):
        for slot in slots:
            whole(slot).wait_recv()

    def ids_across(slot):
        group = next(g for g in TOGETHER if slot in g)[0]
        return remote(cid.at[slot, core], cid.at[slot, core], ids_pair_sent, ids_pair.at[group], sibling)

    def ids(edge):
        src, dst, which = edge
        group = next(g for g in ARRIVING if dst in g)[0]
        return remote(cid.at[src, core], cid.at[dst, core], ids_sent, ids_in.at[group], links[which])

    def got_ids(*slots):
        some = pl.ds(slots[0], len(slots))
        remote(cid.at[some, core], cid.at[some, core], ids_sent, ids_in.at[slots[0]], sibling).wait_recv()
        for slot in slots:
            for e in FIRST + SECOND:
                if e[0] == slot:
                    ids(e).start()
            if slot in SHARED:
                ids_across(slot).start()
        for slot in slots:
            row_ids(slot)

    edge_to = {e[1]: e for e in FIRST + SECOND}

    def row_ids(slot):
        wide = jnp.broadcast_to(cid[slot, core], (128, rows))
        rid[slot] = wide.T

    def compare(columns, pieces, own=False):
        a = jnp.concatenate([buf[i, core, pl.ds(begin, count)] for i, begin, count in pieces], axis=0)
        b = jnp.concatenate([buf[columns, 0], buf[columns, 1]], axis=0)
        s = lax.dot_general(a, b, (((1,), (1,)), ((), ())), preferred_element_type=jnp.float32)
        left = jnp.concatenate([rid[i, pl.ds(begin, count)] for i, begin, count in pieces], axis=0)
        mask = jnp.concatenate([left] * (2 * rows // 128), axis=1) == jnp.concatenate(
            [cid[columns, 0], cid[columns, 1]], axis=1
        )
        if own:
            at = lax.broadcasted_iota(jnp.int32, s.shape, 0) + core * rows
            mask = mask & (at != lax.broadcasted_iota(jnp.int32, s.shape, 1))
        s = jnp.where(mask, s, -1.0)
        best = s[:, :128]
        for q in range(1, 2 * rows // 128):
            best = jnp.maximum(best, s[:, 128 * q : 128 * q + 128])
        row = 0
        for i, begin, count in pieces:
            rowacc[i, pl.ds(begin, count)] = jnp.maximum(rowacc[i, pl.ds(begin, count)], best[row : row + count])
            row += count
        if not own:
            total = jnp.max(s.reshape(s.shape[0] // 8, 8, s.shape[1]), axis=0)
            colacc[columns] = jnp.maximum(colacc[columns], total)

    def full(which):
        return [(i, 0, rows) for i in which]

    def halves(which, h):
        return [(i, h * half, half) for i in which]

    def result(slot, which):
        return remote(outb.at[slot, which], inb.at[slot, core], res_sent, res_in, device(owner(slot), which))

    def result_pair():
        return remote(outb.at[0, 1 - core], inb.at[0, core], res_pair_sent, res_pair_in, sibling)

    def finish(slots):
        for slot in slots:
            down = jnp.max(colacc[slot], axis=0, keepdims=True)
            outb[slot, 0] = down[:, :rows]
            outb[slot, 1] = down[:, rows:]
            along = jnp.max(rowacc[slot].T, axis=0, keepdims=True)
            outb[slot, core] = jnp.maximum(outb[slot, core], along)
            if slot == 0:
                result_pair().start()
            else:
                for which in range(2):
                    result(slot, which).start()

    load_ids.wait()
    cid[0, core] = cluster_ref[...]
    normalise(0)
    pl.semaphore_wait(barrier, len(partners))
    for dst in (1, 2, 3, 4):
        ids(edge_to[dst]).start()
    for n in range(CHUNKS // 4):
        for dst in (1, 2):
            chunk(edge_to[dst], n).start()
    normalise(1)
    for dst in (3, 4):
        part(edge_to[dst], 0).start()
    normalise(2)
    for n in range(CHUNKS // 4, AHEAD):
        for dst in (1, 2):
            chunk(edge_to[dst], n).start()
    normalise(3)
    ids_across(0).start()
    for h in range(2):
        across(0, h).start()
    rowacc[...] = jnp.full(rowacc.shape, -1.0, jnp.float32)
    colacc[...] = jnp.full(colacc.shape, -1.0, jnp.float32)
    row_ids(0)

    for n in range(CHUNKS):
        for dst in (1, 2):
            if n + AHEAD < CHUNKS:
                chunk(edge_to[dst], n + AHEAD).start()
        if n + AHEAD == CHUNKS:
            for dst in (7, 8):
                part(edge_to[dst], 0).start()
        for src, dst in ((1, 5), (2, 6)):
            chunk(edge_to[src], n).wait_recv()
            chunk(edge_to[dst], n).start()
        if n == 0:
            got_ids(1, 2, 3, 4)
        if n == 2:
            for dst in (3, 4):
                part(edge_to[dst], 1).start()
            paired_ids(0)
            paired(0)
            compare(0, full((0,)), own=True)
        if n == HALFWAY:
            for dst in (3, 4):
                got(dst, 0)
            for dst in (9, 10):
                part(edge_to[dst], 0).start()
            for dst in (1, 3, 4):
                across(dst, 0).start()
            got_ids(5, 6)
    for dst in (5, 6):
        got(dst, 0)
    for dst in (11, 12):
        part(edge_to[dst], 0).start()
    for dst in (3, 4):
        got(dst, 1)
    for dst in (7, 8, 9, 10):
        part(edge_to[dst], 1).start()
    for dst in (1, 3, 4):
        across(dst, 1).start()
    for dst in (5, 6):
        across(dst, 0).start()
    paired_ids(1, 3, 4)
    paired(1, 3, 4)
    compare(NEAR[0][0], full(NEAR[0][1]))
    for dst in (5, 6):
        got(dst, 1)
    for dst in (11, 12):
        part(edge_to[dst], 1).start()
    for dst in (5, 6):
        across(dst, 1).start()
    got_ids(7, 8, 9, 10, 11, 12)
    for j, which in NEAR[1:]:
        compare(j, full(which))
    paired_ids(5, 6)
    paired(5, 6)
    for j, which in RELAYED:
        compare(j, full(which))
    finish(DONE_NEAR)

    for h in range(2):
        for dst in (7, 8, 9, 10):
            got(dst, h)
        for dst in (7, 10):
            across(dst, h).start()
        for j, which in FAR:
            compare(j, halves(which, h))
        if h == 1:
            finish(DONE_FAR)
        for dst in (11, 12):
            got(dst, h)
        across(11, h).start()
        for j, which in LAST:
            compare(j, halves(which, h))
    finish(DONE_LAST)
    paired_ids(7, 10, 11)
    paired(7, 10)
    for j, which in LAST_FULL:
        compare(j, full(which))
    finish(DONE_FULL)
    paired(11)
    either, which = LAST_EITHER
    compare(jnp.where(here[0] // 2 == 0, *either), full(which))

    finish(DONE)
    result_pair().wait()
    everything = pltpu.make_async_remote_copy(
        src_ref=outb.at[pl.ds(1, K - 1)], dst_ref=inb.at[pl.ds(1, K - 1)], send_sem=res_sent, recv_sem=res_in,
        device_id=sibling, device_id_type=MESH,
    )
    everything.wait_recv()
    best = jnp.maximum(outb[0, core], inb[0, 1 - core])
    best = jnp.maximum(best, jnp.max(jnp.max(inb[pl.ds(1, K - 1)], axis=0), axis=0))
    out_ref[...] = jnp.maximum(best, -1.0)

    everything.wait_send()
    every, across_all = pl.ds(0, len(FIRST + SECOND)), pl.ds(0, len(SHARED))
    remote(cid.at[every, core], cid.at[every, core], ids_sent, ids_in.at[0], sibling).wait_send()
    remote(buf.at[every, core], buf.at[every, core], sent, arrive.at[0], sibling).wait_send()
    remote(cid.at[across_all, core], cid.at[across_all, core], ids_pair_sent, ids_pair.at[0], sibling).wait_send()
    remote(buf.at[across_all, core], buf.at[across_all, core], sent_pair, shared.at[0], sibling).wait_send()


def per_device(embeddings, cluster):
    rows, width = embeddings.shape
    dma = pltpu.SemaphoreType.DMA
    best = pl.pallas_call(
        kernel,
        out_shape=jax.ShapeDtypeStruct((1, rows), jnp.float32),
        in_specs=[pl.BlockSpec(memory_space=pltpu.HBM)] * 2,
        out_specs=pl.BlockSpec(memory_space=pltpu.VMEM),
        scratch_shapes=[
            pltpu.VMEM((rows, width), embeddings.dtype),
            pltpu.VMEM((1, rows), jnp.int32),
            pltpu.VMEM((K, 2, rows, width), jnp.bfloat16),
            pltpu.VMEM((K, 2, 1, rows), jnp.int32),
            pltpu.VMEM((K, rows, 128), jnp.int32),
            pltpu.VMEM((K, rows, 128), jnp.float32),
            pltpu.VMEM((K, 8, 2 * rows), jnp.float32),
            pltpu.VMEM((K, 2, 1, rows), jnp.float32),
            pltpu.VMEM((K, 2, 1, rows), jnp.float32),
            dma((2 * CHUNKS + 2 * (K - 3),)), dma((K,)), dma((K,)), dma((K,)), dma, dma, dma, dma,
            dma, dma, dma, dma, dma((4,)), dma,
        ],
        compiler_params=pltpu.CompilerParams(
            collective_id=0, has_side_effects=True, vmem_limit_bytes=56 * 2**20
        ),
    )(embeddings, cluster.reshape(1, rows))
    return best.reshape(rows)


def solution(mesh):
    placed = (P(("group", "tile"), None), P(("group", "tile")))
    return jax.shard_map(
        per_device, mesh=mesh, in_specs=placed, out_specs=P(("group", "tile")), check_vma=False
    )
```

```python
import functools

import jax
import jax.numpy as jnp
from jax import lax
from jax.experimental import pallas as pl
from jax.experimental.pallas import tpu as pltpu
from jax.sharding import PartitionSpec as P

EPS = 1e-06
MESH = pl.DeviceIdType.MESH

SLOTS = (
    (0, 0, 0), (1, 0, 0), (3, 0, 0), (0, 1, 0), (0, 0, 1), (1, 3, 0), (3, 0, 3),
    (1, 1, 0), (3, 1, 0), (0, 2, 0), (0, 0, 2), (1, 2, 0), (3, 0, 2),
)
FIRST = ((0, 1, 0), (0, 2, 1), (0, 3, 2), (0, 4, 4), (1, 5, 3), (2, 6, 5))
SECOND = ((3, 7, 0), (3, 8, 1), (3, 9, 2), (4, 10, 4), (5, 11, 3), (6, 12, 5))
DETOUR = ((9, 11, 0), (10, 12, 1))
HEAD = 32
NEAR = ((4, (0, 2, 3)), (3, (0, 2, 1)), (1, (0, 2, 4)))
RELAYED = ((5, (3, 4, 2)), (6, (4, 3, 1, 5)))
FAR = ((0, (10, 9)), (3, (10,)), (5, (10, 8)))
LAST = ((4, (9, 7, 8, 11)), (6, (8, 9, 7, 11)))
LAST_FULL = ((10, (9, 7, 11)), (7, (12,)))
LAST_EITHER = ((1, 11), (12,))
ARRIVING = ((1, 2, 3, 4), (5, 6), (7, 8, 9, 10, 11, 12))
TOGETHER = ((0,), (1, 3, 4), (5, 6), (7, 10, 11))
SHARED = (0, 1, 3, 4, 5, 6, 7, 10, 11)

K = len(SLOTS)
BOUNDS = tuple(range(0, 257, 16))
CHUNKS = len(BOUNDS) - 1
SPLIT = 128
AHEAD = 7


def kernel(x_hbm, cluster_hbm, out_ref, x_ref, cluster_ref, buf, cid, rid, rowacc, colacc, outb, inb,
           arrive, shared, ids_in, ids_pair, sent, sent_pair, ids_sent, ids_pair_sent,
           res_in, res_pair_in, res_sent, res_pair_sent, loaded, loaded_ids):
    rows = x_ref.shape[0]
    limits = (0, SPLIT, rows)
    halfway = BOUNDS.index(SPLIT)
    group, tile = lax.axis_index("group"), lax.axis_index("tile")
    core = lax.rem(group, 2)
    here = (group // 2, tile // 4, lax.rem(tile, 4))
    def device(chip, which):
        return (chip[0] * 2 + which, chip[1] * 4 + chip[2])

    def link(which):
        axis, step = which // 2, 1 - 2 * (which % 2)
        chip = list(here)
        chip[axis] = lax.rem(here[axis] + step + 4, 4)
        return chip

    def owner(slot):
        return [lax.rem(h - s + 4, 4) for h, s in zip(here, SLOTS[slot])]

    sibling = device(here, 1 - core)
    links = [device(link(w), core) for w in range(6)]

    barrier = pltpu.get_barrier_semaphore()
    partners = links + [sibling]
    for partner in partners:
        pl.semaphore_signal(barrier, inc=1, device_id=partner, device_id_type=MESH)

    quarter = rows // 4

    def load(q):
        rows_of = pl.ds(q * quarter, quarter)
        return pltpu.make_async_copy(x_hbm.at[rows_of], x_ref.at[rows_of], loaded.at[q])

    load_ids = pltpu.make_async_copy(cluster_hbm, cluster_ref, loaded_ids)
    load(0).start()
    load_ids.start()
    for q in range(1, 4):
        load(q).start()

    def normalise(q):
        rows_of = pl.ds(q * quarter, quarter)
        load(q).wait()
        e32 = x_ref[rows_of].astype(jnp.float32)
        normed = e32 * lax.rsqrt(jnp.sum(e32 * e32, axis=1, keepdims=True) + EPS)
        buf[0, core, rows_of] = normed.astype(jnp.bfloat16)

    def remote(src, dst, send, recv, to):
        return pltpu.make_async_remote_copy(
            src_ref=src, dst_ref=dst, send_sem=send, recv_sem=recv, device_id=to, device_id_type=MESH
        )

    def piece(begin, end):
        return pl.ds(begin, end - begin)

    def move(edge, rows_of, sem):
        src, dst, which = edge
        return remote(buf.at[src, core, rows_of], buf.at[dst, core, rows_of], sent, sem, links[which])

    def chunk(edge, n):
        dst = edge[1]
        sem = arrive.at[(dst - 1) * CHUNKS + n if dst in (1, 2) else 2 * CHUNKS + 2 * (dst - 3) + n // halfway]
        return move(edge, piece(BOUNDS[n], BOUNDS[n + 1]), sem)

    def part(edge, h):
        begin = HEAD if edge[1] in (11, 12) and h == 0 else limits[h]
        return move(edge, piece(begin, limits[h + 1]), arrive.at[2 * CHUNKS + 2 * (edge[1] - 3) + h])

    def detour(edge):
        return move(edge, piece(0, HEAD), arrive.at[2 * CHUNKS + 2 * (K - 3) + edge[1] - 11])

    def got(slot, h):
        part((0, slot, 0), h).wait_recv()

    def across(slot, h):
        return across_rows(slot, piece(HEAD if slot == 11 and h == 0 else limits[h], limits[h + 1]))

    def across_rows(slot, rows_of):
        return remote(buf.at[slot, core, rows_of], buf.at[slot, core, rows_of], sent_pair, shared.at[slot], sibling)

    def whole(slot):
        return remote(buf.at[slot, core], buf.at[slot, core], sent_pair, shared.at[slot], sibling)

    def paired_ids(*slots):
        some = pl.ds(0, len(slots))
        remote(cid.at[some, core], cid.at[some, core], ids_pair_sent, ids_pair.at[slots[0]], sibling).wait_recv()

    def paired(*slots):
        for slot in slots:
            whole(slot).wait_recv()

    def ids_across(slot):
        group = next(g for g in TOGETHER if slot in g)[0]
        return remote(cid.at[slot, core], cid.at[slot, core], ids_pair_sent, ids_pair.at[group], sibling)

    def ids(edge):
        src, dst, which = edge
        group = next(g for g in ARRIVING if dst in g)[0]
        return remote(cid.at[src, core], cid.at[dst, core], ids_sent, ids_in.at[group], links[which])

    def got_ids(*slots):
        some = pl.ds(slots[0], len(slots))
        remote(cid.at[some, core], cid.at[some, core], ids_sent, ids_in.at[slots[0]], sibling).wait_recv()
        for slot in slots:
            for e in FIRST + SECOND:
                if e[0] == slot:
                    ids(e).start()
            if slot in SHARED:
                ids_across(slot).start()
        for slot in slots:
            row_ids(slot)

    edge_to = {e[1]: e for e in FIRST + SECOND}

    def row_ids(slot):
        wide = jnp.broadcast_to(cid[slot, core], (128, rows))
        rid[slot] = wide.T

    def compare(columns, pieces, own=False):
        a = jnp.concatenate([buf[i, core, pl.ds(begin, count)] for i, begin, count in pieces], axis=0)
        b = jnp.concatenate([buf[columns, 0], buf[columns, 1]], axis=0)
        s = lax.dot_general(a, b, (((1,), (1,)), ((), ())), preferred_element_type=jnp.float32)
        left = jnp.concatenate([rid[i, pl.ds(begin, count)] for i, begin, count in pieces], axis=0)
        mask = jnp.concatenate([left] * (2 * rows // 128), axis=1) == jnp.concatenate(
            [cid[columns, 0], cid[columns, 1]], axis=1
        )
        if own:
            at = lax.broadcasted_iota(jnp.int32, s.shape, 0) + core * rows
            mask = mask & (at != lax.broadcasted_iota(jnp.int32, s.shape, 1))
        s = jnp.where(mask, s, -1.0)
        best = s[:, :128]
        for q in range(1, 2 * rows // 128):
            best = jnp.maximum(best, s[:, 128 * q : 128 * q + 128])
        row = 0
        for i, begin, count in pieces:
            rowacc[i, pl.ds(begin, count)] = jnp.maximum(rowacc[i, pl.ds(begin, count)], best[row : row + count])
            row += count
        if not own:
            total = jnp.max(s.reshape(s.shape[0] // 8, 8, s.shape[1]), axis=0)
            colacc[columns] = jnp.maximum(colacc[columns], total)

    def full(which):
        return [(i, 0, rows) for i in which]

    def halves(which, h):
        return [(i, limits[h], limits[h + 1] - limits[h]) for i in which]

    def result(slot, which):
        return remote(outb.at[slot, which], inb.at[slot, core], res_sent, res_in, device(owner(slot), which))

    def result_pair():
        return remote(outb.at[0, 1 - core], inb.at[0, core], res_pair_sent, res_pair_in, sibling)

    def finish(slots):
        for slot in slots:
            down = jnp.max(colacc[slot], axis=0, keepdims=True)
            outb[slot, 0] = down[:, :rows]
            outb[slot, 1] = down[:, rows:]
            along = jnp.max(rowacc[slot].T, axis=0, keepdims=True)
            outb[slot, core] = jnp.maximum(outb[slot, core], along)
            if slot == 0:
                result_pair().start()
            else:
                for which in range(2):
                    result(slot, which).start()

    load_ids.wait()
    cid[0, core] = cluster_ref[...]
    normalise(0)
    pl.semaphore_wait(barrier, len(partners))
    for dst in (1, 2, 3, 4):
        ids(edge_to[dst]).start()
    for n in range(CHUNKS // 4):
        for dst in (1, 2):
            chunk(edge_to[dst], n).start()
    normalise(1)
    for dst in (3, 4):
        part(edge_to[dst], 0).start()
    normalise(2)
    for n in range(CHUNKS // 4, AHEAD):
        for dst in (1, 2):
            chunk(edge_to[dst], n).start()
    normalise(3)
    ids_across(0).start()
    for h in range(2):
        across(0, h).start()
    rowacc[...] = jnp.full(rowacc.shape, -1.0, jnp.float32)
    colacc[...] = jnp.full(colacc.shape, -1.0, jnp.float32)
    row_ids(0)

    for n in range(CHUNKS):
        for dst in (1, 2):
            if n + AHEAD < CHUNKS:
                chunk(edge_to[dst], n + AHEAD).start()
        for src, dst in ((1, 5), (2, 6)):
            chunk(edge_to[src], n).wait_recv()
            chunk(edge_to[dst], n).start()
        if n == 0:
            got_ids(1, 2, 3, 4)
        if n == 2:
            for dst in (3, 4):
                part(edge_to[dst], 1).start()
            paired_ids(0)
            paired(0)
            compare(0, full((0,)), own=True)
        if n == halfway:
            for dst in (3, 4):
                got(dst, 0)
            for dst in (7, 8, 9, 10):
                part(edge_to[dst], 0).start()
            for dst in (1, 3, 4):
                across(dst, 0).start()
            got_ids(5, 6)
    for dst in (5, 6):
        got(dst, 0)
    for dst in (11, 12):
        part(edge_to[dst], 0).start()
    for dst in (3, 4):
        got(dst, 1)
    for dst in (7, 8, 9, 10):
        part(edge_to[dst], 1).start()
    for dst in (1, 3, 4):
        across(dst, 1).start()
    for dst in (5, 6):
        across(dst, 0).start()
    paired_ids(1, 3, 4)
    paired(1, 3, 4)
    compare(NEAR[0][0], full(NEAR[0][1]))
    for dst in (5, 6):
        got(dst, 1)
    for dst in (11, 12):
        part(edge_to[dst], 1).start()
    for dst in (5, 6):
        across(dst, 1).start()
    got_ids(7, 8, 9, 10, 11, 12)
    for j, which in NEAR[1:]:
        compare(j, full(which))
    paired_ids(5, 6)
    paired(5, 6)
    for j, which in RELAYED:
        compare(j, full(which))
    finish((2,))

    for h in range(2):
        for dst in (7, 8, 9, 10):
            got(dst, h)
        if h == 0:
            for edge in DETOUR:
                detour(edge).start()
        for dst in (7, 10):
            across(dst, h).start()
        for j, which in FAR:
            compare(j, halves(which, h))
        for dst in (11, 12):
            got(dst, h)
        if h == 1:
            for edge in DETOUR:
                detour(edge).wait_recv()
            across_rows(11, piece(0, HEAD)).start()
        across(11, h).start()
        for j, which in LAST:
            pieces = halves([i for i in which if i != 11], h)
            if h == 0:
                pieces += [(11, HEAD, SPLIT - HEAD)]
            else:
                pieces += [(11, SPLIT, rows - SPLIT), (11, 0, HEAD)]
            compare(j, pieces)
    paired_ids(7, 10, 11)
    paired(7, 10)
    for j, which in LAST_FULL:
        compare(j, full(which))
    paired(11)
    either, which = LAST_EITHER
    compare(jnp.where(here[0] // 2 == 0, *either), full(which))
    finish((11, 12, 10, 9, 8, 7, 6, 5, 1, 3, 4, 0))

    result_pair().wait()
    everything = pltpu.make_async_remote_copy(
        src_ref=outb.at[pl.ds(1, K - 1)], dst_ref=inb.at[pl.ds(1, K - 1)], send_sem=res_sent, recv_sem=res_in,
        device_id=sibling, device_id_type=MESH,
    )
    everything.wait_recv()
    best = jnp.maximum(outb[0, core], inb[0, 1 - core])
    best = jnp.maximum(best, jnp.max(jnp.max(inb[pl.ds(1, K - 1)], axis=0), axis=0))
    out_ref[...] = jnp.maximum(best, -1.0)

    everything.wait_send()
    every, across_all = pl.ds(0, len(FIRST + SECOND)), pl.ds(0, len(SHARED))
    remote(cid.at[every, core], cid.at[every, core], ids_sent, ids_in.at[0], sibling).wait_send()
    remote(buf.at[every, core], buf.at[every, core], sent, arrive.at[0], sibling).wait_send()
    remote(cid.at[across_all, core], cid.at[across_all, core], ids_pair_sent, ids_pair.at[0], sibling).wait_send()
    remote(buf.at[across_all, core], buf.at[across_all, core], sent_pair, shared.at[0], sibling).wait_send()


def per_device(embeddings, cluster):
    rows, width = embeddings.shape
    dma = pltpu.SemaphoreType.DMA
    best = pl.pallas_call(
        kernel,
        out_shape=jax.ShapeDtypeStruct((1, rows), jnp.float32),
        in_specs=[pl.BlockSpec(memory_space=pltpu.HBM)] * 2,
        out_specs=pl.BlockSpec(memory_space=pltpu.VMEM),
        scratch_shapes=[
            pltpu.VMEM((rows, width), embeddings.dtype),
            pltpu.VMEM((1, rows), jnp.int32),
            pltpu.VMEM((K, 2, rows, width), jnp.bfloat16),
            pltpu.VMEM((K, 2, 1, rows), jnp.int32),
            pltpu.VMEM((K, rows, 128), jnp.int32),
            pltpu.VMEM((K, rows, 128), jnp.float32),
            pltpu.VMEM((K, 8, 2 * rows), jnp.float32),
            pltpu.VMEM((K, 2, 1, rows), jnp.float32),
            pltpu.VMEM((K, 2, 1, rows), jnp.float32),
            dma((2 * CHUNKS + 2 * (K - 3) + 2,)), dma((K,)), dma((K,)), dma((K,)), dma, dma, dma, dma,
            dma, dma, dma, dma, dma((4,)), dma,
        ],
        compiler_params=pltpu.CompilerParams(
            collective_id=0, has_side_effects=True, vmem_limit_bytes=56 * 2**20
        ),
    )(embeddings, cluster.reshape(1, rows))
    return best.reshape(rows)


def solution(mesh):
    placed = (P(("group", "tile"), None), P(("group", "tile")))
    return jax.shard_map(
        per_device, mesh=mesh, in_specs=placed, out_specs=P(("group", "tile")), check_vma=False
    )
```

```python
import functools

import jax
import jax.numpy as jnp
from jax import lax
from jax.experimental import pallas as pl
from jax.experimental.pallas import tpu as pltpu
from jax.sharding import PartitionSpec as P

EPS = 1e-06
MESH = pl.DeviceIdType.MESH

SLOTS = (
    (0, 0, 0), (1, 0, 0), (3, 0, 0), (0, 1, 0), (0, 0, 1), (1, 3, 0), (3, 0, 3),
    (1, 1, 0), (3, 1, 0), (0, 2, 0), (0, 0, 2), (1, 2, 0), (3, 0, 2),
)
FIRST = ((0, 1, 0), (0, 2, 1), (0, 3, 2), (0, 4, 4), (1, 5, 3), (2, 6, 5))
SECOND = ((3, 7, 0), (3, 8, 1), (3, 9, 2), (4, 10, 4), (5, 11, 3), (6, 12, 5))
DETOUR = ((9, 11, 0), (10, 12, 1))
HEAD = 32
NEAR = ((4, (0, 2, 3)), (3, (0, 2, 1)), (1, (0, 2, 4)))
RELAYED = ((5, (3, 4, 2)), (6, (4, 3, 1, 5)))
FAR = ((0, (10, 9)), (3, (10,)), (5, (10, 8)))
LAST = ((4, (9, 7, 8, 11)), (6, (8, 9, 7, 11)))
BEFORE_LAST = ((10, (9, 7)),)
LAST_FULL = ((10, (11,)), (7, (12,)))
LAST_EITHER = ((1, 11), (12,))
ARRIVING = ((1, 2, 3, 4), (5, 6), (7, 8, 9, 10, 11, 12))
TOGETHER = ((0,), (1, 3, 4), (5, 6), (7, 10, 11))
SHARED = (0, 1, 3, 4, 5, 6, 7, 10, 11)

K = len(SLOTS)
BOUNDS = tuple(range(0, 257, 16))
CHUNKS = len(BOUNDS) - 1
SPLIT = 128
AHEAD = 7


def kernel(x_hbm, cluster_hbm, out_ref, x_ref, cluster_ref, buf, cid, rid, rowacc, colacc, outb, inb,
           arrive, shared, ids_in, ids_pair, sent, sent_pair, ids_sent, ids_pair_sent,
           res_in, res_pair_in, res_sent, res_pair_sent, loaded, loaded_ids):
    rows = x_ref.shape[0]
    limits = (0, SPLIT, rows)
    halfway = BOUNDS.index(SPLIT)
    group, tile = lax.axis_index("group"), lax.axis_index("tile")
    core = lax.rem(group, 2)
    here = (group // 2, tile // 4, lax.rem(tile, 4))
    def device(chip, which):
        return (chip[0] * 2 + which, chip[1] * 4 + chip[2])

    def link(which):
        axis, step = which // 2, 1 - 2 * (which % 2)
        chip = list(here)
        chip[axis] = lax.rem(here[axis] + step + 4, 4)
        return chip

    def owner(slot):
        return [lax.rem(h - s + 4, 4) for h, s in zip(here, SLOTS[slot])]

    sibling = device(here, 1 - core)
    links = [device(link(w), core) for w in range(6)]

    barrier = pltpu.get_barrier_semaphore()
    partners = links + [sibling]
    for partner in partners:
        pl.semaphore_signal(barrier, inc=1, device_id=partner, device_id_type=MESH)

    quarter = rows // 4

    def load(q):
        rows_of = pl.ds(q * quarter, quarter)
        return pltpu.make_async_copy(x_hbm.at[rows_of], x_ref.at[rows_of], loaded.at[q])

    load_ids = pltpu.make_async_copy(cluster_hbm, cluster_ref, loaded_ids)
    load(0).start()
    load_ids.start()
    for q in range(1, 4):
        load(q).start()

    def normalise(q):
        rows_of = pl.ds(q * quarter, quarter)
        load(q).wait()
        e32 = x_ref[rows_of].astype(jnp.float32)
        normed = e32 * lax.rsqrt(jnp.sum(e32 * e32, axis=1, keepdims=True) + EPS)
        buf[0, core, rows_of] = normed.astype(jnp.bfloat16)

    def remote(src, dst, send, recv, to):
        return pltpu.make_async_remote_copy(
            src_ref=src, dst_ref=dst, send_sem=send, recv_sem=recv, device_id=to, device_id_type=MESH
        )

    def piece(begin, end):
        return pl.ds(begin, end - begin)

    def move(edge, rows_of, sem):
        src, dst, which = edge
        return remote(buf.at[src, core, rows_of], buf.at[dst, core, rows_of], sent, sem, links[which])

    def chunk(edge, n):
        dst = edge[1]
        sem = arrive.at[(dst - 1) * CHUNKS + n if dst in (1, 2) else 2 * CHUNKS + 2 * (dst - 3) + n // halfway]
        return move(edge, piece(BOUNDS[n], BOUNDS[n + 1]), sem)

    def part(edge, h):
        begin = HEAD if edge[1] in (11, 12) and h == 0 else limits[h]
        return move(edge, piece(begin, limits[h + 1]), arrive.at[2 * CHUNKS + 2 * (edge[1] - 3) + h])

    def detour(edge):
        return move(edge, piece(0, HEAD), arrive.at[2 * CHUNKS + 2 * (K - 3) + edge[1] - 11])

    def got(slot, h):
        part((0, slot, 0), h).wait_recv()

    def across(slot, h):
        return across_rows(slot, piece(HEAD if slot == 11 and h == 0 else limits[h], limits[h + 1]))

    def across_rows(slot, rows_of):
        return remote(buf.at[slot, core, rows_of], buf.at[slot, core, rows_of], sent_pair, shared.at[slot], sibling)

    def whole(slot):
        return remote(buf.at[slot, core], buf.at[slot, core], sent_pair, shared.at[slot], sibling)

    def paired_ids(*slots):
        some = pl.ds(0, len(slots))
        remote(cid.at[some, core], cid.at[some, core], ids_pair_sent, ids_pair.at[slots[0]], sibling).wait_recv()

    def paired(*slots):
        for slot in slots:
            whole(slot).wait_recv()

    def ids_across(slot):
        group = next(g for g in TOGETHER if slot in g)[0]
        return remote(cid.at[slot, core], cid.at[slot, core], ids_pair_sent, ids_pair.at[group], sibling)

    def ids(edge):
        src, dst, which = edge
        group = next(g for g in ARRIVING if dst in g)[0]
        return remote(cid.at[src, core], cid.at[dst, core], ids_sent, ids_in.at[group], links[which])

    def got_ids(*slots):
        some = pl.ds(slots[0], len(slots))
        remote(cid.at[some, core], cid.at[some, core], ids_sent, ids_in.at[slots[0]], sibling).wait_recv()
        for slot in slots:
            for e in FIRST + SECOND:
                if e[0] == slot:
                    ids(e).start()
            if slot in SHARED:
                ids_across(slot).start()
        for slot in slots:
            row_ids(slot)

    edge_to = {e[1]: e for e in FIRST + SECOND}

    def row_ids(slot):
        wide = jnp.broadcast_to(cid[slot, core], (128, rows))
        rid[slot] = wide.T

    def compare(columns, pieces, own=False):
        a = jnp.concatenate([buf[i, core, pl.ds(begin, count)] for i, begin, count in pieces], axis=0)
        b = jnp.concatenate([buf[columns, 0], buf[columns, 1]], axis=0)
        s = lax.dot_general(a, b, (((1,), (1,)), ((), ())), preferred_element_type=jnp.float32)
        left = jnp.concatenate([rid[i, pl.ds(begin, count)] for i, begin, count in pieces], axis=0)
        mask = jnp.concatenate([left] * (2 * rows // 128), axis=1) == jnp.concatenate(
            [cid[columns, 0], cid[columns, 1]], axis=1
        )
        if own:
            at = lax.broadcasted_iota(jnp.int32, s.shape, 0) + core * rows
            mask = mask & (at != lax.broadcasted_iota(jnp.int32, s.shape, 1))
        s = jnp.where(mask, s, -1.0)
        best = s[:, :128]
        for q in range(1, 2 * rows // 128):
            best = jnp.maximum(best, s[:, 128 * q : 128 * q + 128])
        row = 0
        for i, begin, count in pieces:
            rowacc[i, pl.ds(begin, count)] = jnp.maximum(rowacc[i, pl.ds(begin, count)], best[row : row + count])
            row += count
        if not own:
            total = jnp.max(s.reshape(s.shape[0] // 8, 8, s.shape[1]), axis=0)
            colacc[columns] = jnp.maximum(colacc[columns], total)

    def full(which):
        return [(i, 0, rows) for i in which]

    def halves(which, h):
        return [(i, limits[h], limits[h + 1] - limits[h]) for i in which]

    def result(slot, which):
        return remote(outb.at[slot, which], inb.at[slot, core], res_sent, res_in, device(owner(slot), which))

    def result_pair():
        return remote(outb.at[0, 1 - core], inb.at[0, core], res_pair_sent, res_pair_in, sibling)

    def finish(slots):
        for slot in slots:
            down = jnp.max(colacc[slot], axis=0, keepdims=True)
            outb[slot, 0] = down[:, :rows]
            outb[slot, 1] = down[:, rows:]
            along = jnp.max(rowacc[slot].T, axis=0, keepdims=True)
            outb[slot, core] = jnp.maximum(outb[slot, core], along)
            if slot == 0:
                result_pair().start()
            else:
                for which in range(2):
                    result(slot, which).start()

    load_ids.wait()
    cid[0, core] = cluster_ref[...]
    normalise(0)
    pl.semaphore_wait(barrier, len(partners))
    for dst in (1, 2, 3, 4):
        ids(edge_to[dst]).start()
    for n in range(CHUNKS // 4):
        for dst in (1, 2):
            chunk(edge_to[dst], n).start()
    normalise(1)
    for dst in (3, 4):
        part(edge_to[dst], 0).start()
    normalise(2)
    for n in range(CHUNKS // 4, AHEAD):
        for dst in (1, 2):
            chunk(edge_to[dst], n).start()
    normalise(3)
    ids_across(0).start()
    for h in range(2):
        across(0, h).start()
    rowacc[...] = jnp.full(rowacc.shape, -1.0, jnp.float32)
    colacc[...] = jnp.full(colacc.shape, -1.0, jnp.float32)
    row_ids(0)

    for n in range(CHUNKS):
        for dst in (1, 2):
            if n + AHEAD < CHUNKS:
                chunk(edge_to[dst], n + AHEAD).start()
        for src, dst in ((1, 5), (2, 6)):
            chunk(edge_to[src], n).wait_recv()
            chunk(edge_to[dst], n).start()
        if n == 0:
            got_ids(1, 2, 3, 4)
        if n == 2:
            for dst in (3, 4):
                part(edge_to[dst], 1).start()
            paired_ids(0)
            paired(0)
            compare(0, full((0,)), own=True)
        if n == halfway:
            for dst in (3, 4):
                got(dst, 0)
            for dst in (7, 8, 9, 10):
                part(edge_to[dst], 0).start()
            for dst in (1, 3, 4):
                across(dst, 0).start()
            got_ids(5, 6)
    for dst in (5, 6):
        got(dst, 0)
    for dst in (11, 12):
        part(edge_to[dst], 0).start()
    for dst in (3, 4):
        got(dst, 1)
    for dst in (7, 8, 9, 10):
        part(edge_to[dst], 1).start()
    for dst in (1, 3, 4):
        across(dst, 1).start()
    for dst in (5, 6):
        across(dst, 0).start()
    paired_ids(1, 3, 4)
    paired(1, 3, 4)
    compare(NEAR[0][0], full(NEAR[0][1]))
    for dst in (5, 6):
        got(dst, 1)
    for dst in (11, 12):
        part(edge_to[dst], 1).start()
    for dst in (5, 6):
        across(dst, 1).start()
    got_ids(7, 8, 9, 10, 11, 12)
    for j, which in NEAR[1:]:
        compare(j, full(which))
    paired_ids(5, 6)
    paired(5, 6)
    for j, which in RELAYED:
        compare(j, full(which))
    finish((2,))

    for h in range(2):
        for dst in (7, 8, 9, 10):
            got(dst, h)
        if h == 0:
            for edge in DETOUR:
                detour(edge).start()
        for dst in (7, 10):
            across(dst, h).start()
        for j, which in FAR:
            compare(j, halves(which, h))
        if h == 1:
            paired_ids(7, 10, 11)
            paired(7, 10)
            for j, which in BEFORE_LAST:
                compare(j, full(which))
        for dst in (11, 12):
            got(dst, h)
        if h == 1:
            for edge in DETOUR:
                detour(edge).wait_recv()
            across_rows(11, piece(0, HEAD)).start()
        across(11, h).start()
        for j, which in LAST:
            pieces = halves([i for i in which if i != 11], h)
            if h == 0:
                pieces += [(11, HEAD, SPLIT - HEAD)]
            else:
                pieces += [(11, SPLIT, rows - SPLIT), (11, 0, HEAD)]
            compare(j, pieces)
    for j, which in LAST_FULL:
        compare(j, full(which))
    paired(11)
    either, which = LAST_EITHER
    compare(jnp.where(here[0] // 2 == 0, *either), full(which))
    finish((11, 12, 10, 9, 8, 7, 6, 5, 1, 3, 4, 0))

    result_pair().wait()
    everything = pltpu.make_async_remote_copy(
        src_ref=outb.at[pl.ds(1, K - 1)], dst_ref=inb.at[pl.ds(1, K - 1)], send_sem=res_sent, recv_sem=res_in,
        device_id=sibling, device_id_type=MESH,
    )
    everything.wait_recv()
    best = jnp.maximum(outb[0, core], inb[0, 1 - core])
    best = jnp.maximum(best, jnp.max(jnp.max(inb[pl.ds(1, K - 1)], axis=0), axis=0))
    out_ref[...] = jnp.maximum(best, -1.0)

    everything.wait_send()
    every, across_all = pl.ds(0, len(FIRST + SECOND)), pl.ds(0, len(SHARED))
    remote(cid.at[every, core], cid.at[every, core], ids_sent, ids_in.at[0], sibling).wait_send()
    remote(buf.at[every, core], buf.at[every, core], sent, arrive.at[0], sibling).wait_send()
    remote(cid.at[across_all, core], cid.at[across_all, core], ids_pair_sent, ids_pair.at[0], sibling).wait_send()
    remote(buf.at[across_all, core], buf.at[across_all, core], sent_pair, shared.at[0], sibling).wait_send()


def per_device(embeddings, cluster):
    rows, width = embeddings.shape
    dma = pltpu.SemaphoreType.DMA
    best = pl.pallas_call(
        kernel,
        out_shape=jax.ShapeDtypeStruct((1, rows), jnp.float32),
        in_specs=[pl.BlockSpec(memory_space=pltpu.HBM)] * 2,
        out_specs=pl.BlockSpec(memory_space=pltpu.VMEM),
        scratch_shapes=[
            pltpu.VMEM((rows, width), embeddings.dtype),
            pltpu.VMEM((1, rows), jnp.int32),
            pltpu.VMEM((K, 2, rows, width), jnp.bfloat16),
            pltpu.VMEM((K, 2, 1, rows), jnp.int32),
            pltpu.VMEM((K, rows, 128), jnp.int32),
            pltpu.VMEM((K, rows, 128), jnp.float32),
            pltpu.VMEM((K, 8, 2 * rows), jnp.float32),
            pltpu.VMEM((K, 2, 1, rows), jnp.float32),
            pltpu.VMEM((K, 2, 1, rows), jnp.float32),
            dma((2 * CHUNKS + 2 * (K - 3) + 2,)), dma((K,)), dma((K,)), dma((K,)), dma, dma, dma, dma,
            dma, dma, dma, dma, dma((4,)), dma,
        ],
        compiler_params=pltpu.CompilerParams(
            collective_id=0, has_side_effects=True, vmem_limit_bytes=56 * 2**20
        ),
    )(embeddings, cluster.reshape(1, rows))
    return best.reshape(rows)


def solution(mesh):
    placed = (P(("group", "tile"), None), P(("group", "tile")))
    return jax.shard_map(
        per_device, mesh=mesh, in_specs=placed, out_specs=P(("group", "tile")), check_vma=False
    )
```
